32 devices in a mesh: parts: 2 (over y), dp: 4 (over x, core), tensor: 4 (over z).
Axes of the slice: x: 2, y: 2, z: 4, core: 2. Of those that a mesh axis runs over, the one named last changes fastest.
Arguments:
- acts: bfloat16 [4096, 4096], P(('parts', 'dp'), 'tensor'), parts along dimension 0, may hold values from -6 to 6
- out_grad: bfloat16 [4096, 4096], P(('parts', 'dp'), 'tensor'), parts along dimension 0, may hold values from -6 to 6
- lengths: int32 [16], P(('parts', 'dp')), parts along dimension 0, may hold values from 64 to 256, as said below
- w_gate: bfloat16 [4096, 14336], P('dp', 'tensor'), may hold values from -0.09375 to 0.09375
- w_up: bfloat16 [4096, 14336], P('dp', 'tensor'), may hold values from -0.09375 to 0.09375
- w_down_t: bfloat16 [4096, 14336], P('dp', 'tensor'), may hold values from -0.09375 to 0.09375
- d_proj: bfloat16 [3, 4096, 64], replicated, may hold values from -0.09375 to 0.09375
- ff_proj: bfloat16 [3, 14336, 64], P(None, 'tensor'), may hold values from -0.046875 to 0.046875
- queries: bfloat16 [128, 12288], P(('dp', 'tensor')), may hold values from -0.0068359375 to 0.0068359375
Outputs:
- scores: float32 [16, 4, 32], P(('parts', 'dp'), None, 'tensor'), parts along dimension 0
The draws below stay inside these ranges and needn't reach their ends.
There are 2 independent parts, one for each index of `parts`. The reference program is written for one: setup_inputs(seed, part) draws one part's arguments, and reference() takes and returns one part's arrays. A program takes and returns all parts, laid end to end along the dimension named above; an argument that names none is the same for every part. Nothing has to cross between parts.
Inputs may be any that keep to these rules, and one draw needn't show every extreme that they name: `lengths`: every sequence has at least 64 valid tokens, and some sequence of each part has all 256.
All inputs are finite; a program needn't handle non-finite values.
Results may differ from the reference program's by a relative error of at most 0.0042.
Values may be sent and summed in bfloat16 or wider, within the bound.
No kernel may reach another device: no remote copies, remote signals or barrier semaphores. Data moves between devices by JAX's collectives and lax.ppermute only.
A program may use at most 256 MiB of HBM per device.

```python
import jax
import jax.numpy as jnp
from jax import lax

D = 4096
FF = 14336
RANK = 64
LEN = 256
SEQS = 8
TOKENS = 2048
QUERIES = 128
FEATS = 12288
N_DP = 4


def draw_lengths(key, part):
    key = jax.random.fold_in(key, 5)
    first_key, second_key = jax.random.split(key)
    values = jax.random.randint(first_key, (SEQS,), LEN // 4, LEN + 1)
    full_index = jax.random.randint(second_key, (), 0, SEQS)
    return jnp.where(jnp.arange(SEQS) == full_index, LEN, values).astype(jnp.int32)


def block_scale(key, shape, shards, low, high):
    factor_of, own = 1.0, jax.random.fold_in(key, 6)
    for axis_at, parts in shards:
        heights = jnp.exp(jax.random.uniform(jax.random.fold_in(own, axis_at), (parts,), jnp.float32, low / len(shards), high / len(shards)))
        factor_of = factor_of * jnp.repeat(heights, shape[axis_at] // parts).reshape([-1 if axis == axis_at else 1 for axis in range(len(shape))])
    return factor_of


def normal_values(stream_key, dims, width, bound, cuts=(), held_as=jnp.bfloat16):
    result = jax.random.normal(stream_key, dims, jnp.float32) * width
    if len(cuts) > 0:
        result = block_scale(stream_key, dims, cuts, -0.22, 0.18) * result
    return jnp.clip(result, min=-bound, max=bound).astype(held_as)


def setup_inputs(seed: int = 0, part: int = 0) -> dict:
    arg_keys = jax.random.split(jax.random.key(seed), 10)
    part_keys = jax.random.split(jax.random.fold_in(arg_keys[9], part), 10)
    return {
        "acts": normal_values(part_keys[0], (TOKENS, D), 1.0, 6.0, ((0, 4), (1, 4))),
        "out_grad": normal_values(part_keys[1], (TOKENS, D), 1.0, 6.0, ((0, 4), (1, 4))),
        "lengths": draw_lengths(jax.random.fold_in(jax.random.fold_in(arg_keys[9], part), 71), part),
        "w_gate": normal_values(arg_keys[3], (D, FF), D ** -0.5, 0.09375, ((0, 4), (1, 4))),
        "w_up": normal_values(arg_keys[4], (D, FF), D ** -0.5, 0.09375, ((0, 4), (1, 4))),
        "w_down_t": normal_values(arg_keys[5], (D, FF), D ** -0.5, 0.09375, ((0, 4), (1, 4))),
        "d_proj": normal_values(arg_keys[6], (3, D, RANK), D ** -0.5, 0.09375),
        "ff_proj": normal_values(arg_keys[7], (3, FF, RANK), FF ** -0.5, 0.046875, ((1, 4),)),
        "queries": normal_values(arg_keys[8], (QUERIES, FEATS), (64 * FEATS) ** -0.5, 0.0068359375, ((0, 16),)),
    }


def outer_sum(left, right):
    left_seq = left.reshape(SEQS, LEN, RANK)
    right_seq = right.reshape(SEQS, LEN, RANK)
    return jnp.einsum("slr,slk->srk", left_seq, right_seq, precision=lax.Precision.HIGHEST)


def reference(acts, out_grad, lengths, w_gate, w_up, w_down_t, d_proj, ff_proj, queries):
    positions = jnp.arange(LEN, dtype=jnp.int32)
    keep_mask = (positions[None, :] < lengths[:, None]).astype(jnp.bfloat16).reshape(TOKENS, 1)
    masked_grad = out_grad * keep_mask
    gate_pre = jnp.dot(acts, w_gate, preferred_element_type=jnp.float32)
    up_pre = jnp.dot(acts, w_up, preferred_element_type=jnp.float32)
    sigmoid_gate = jax.nn.sigmoid(gate_pre)
    silu_gate = gate_pre * sigmoid_gate
    hidden = (silu_gate * up_pre).astype(jnp.bfloat16)
    back_grad = jnp.dot(masked_grad, w_down_t, preferred_element_type=jnp.float32)
    grad_gate = (back_grad * up_pre * sigmoid_gate * (1.0 + gate_pre * (1.0 - sigmoid_gate))).astype(jnp.bfloat16)
    grad_up = (back_grad * silu_gate).astype(jnp.bfloat16)
    left_gate = jnp.dot(acts, d_proj[0], preferred_element_type=jnp.float32)
    left_up = jnp.dot(acts, d_proj[1], preferred_element_type=jnp.float32)
    right_down = jnp.dot(masked_grad, d_proj[2], preferred_element_type=jnp.float32)
    right_gate = jnp.dot(grad_gate, ff_proj[0], preferred_element_type=jnp.float32)
    right_up = jnp.dot(grad_up, ff_proj[1], preferred_element_type=jnp.float32)
    left_down = jnp.dot(hidden, ff_proj[2], preferred_element_type=jnp.float32)
    seq_proj = jnp.stack([outer_sum(left_gate, right_gate), outer_sum(left_up, right_up), outer_sum(left_down, right_down)], axis=1)
    proj_b = seq_proj.reshape(SEQS, FEATS).astype(jnp.bfloat16)
    flat_scores = lax.dot_general(proj_b, queries, (((1,), (1,)), ((), ())), preferred_element_type=jnp.float32)
    return flat_scores.reshape(SEQS, N_DP, QUERIES // N_DP)
```

```python
import jax
import jax.numpy as jnp
from jax import lax
from jax.experimental import pallas as pl
from jax.experimental.pallas import tpu as pltpu
from jax.sharding import PartitionSpec as P

HIGHEST = lax.Precision.HIGHEST


def dot(left, right):
    return jnp.dot(left, right, preferred_element_type=jnp.float32)


def activations(gate_pre, up_pre, back_grad):
    sigmoid_gate = jax.nn.sigmoid(gate_pre)
    silu_gate = gate_pre * sigmoid_gate
    hidden = (silu_gate * up_pre).astype(jnp.bfloat16)
    grad_gate = (
        back_grad * up_pre * sigmoid_gate * (1.0 + gate_pre * (1.0 - sigmoid_gate))
    ).astype(jnp.bfloat16)
    grad_up = (back_grad * silu_gate).astype(jnp.bfloat16)
    return hidden, grad_gate, grad_up


def outer_sum(left, right, length):
    rank = left.shape[1]
    left_seq = left.reshape(-1, length, rank)
    right_seq = right.reshape(-1, length, rank)
    return jnp.einsum("slr,slk->srk", left_seq, right_seq, precision=HIGHEST)


def mask_tokens(out_grad, lengths):
    length = out_grad.shape[0] // lengths.shape[0]
    positions = jnp.arange(length, dtype=jnp.int32)
    keep = positions[None, :] < lengths[:, None]
    return out_grad * keep.astype(out_grad.dtype).reshape(-1, 1)


def gathered_body(acts, out_grad, lengths, w_gate, w_up, w_down_t, d_proj, ff_proj, queries):
    seq_dev = lengths.shape[0]
    length = acts.shape[0] // seq_dev
    rank = d_proj.shape[2]
    full_acts = lax.all_gather(acts, "tensor", axis=1, tiled=True)
    masked_grad = lax.all_gather(mask_tokens(out_grad, lengths), "tensor", axis=1, tiled=True)
    gate_pre = dot(full_acts, lax.all_gather(w_gate, "dp", axis=0, tiled=True))
    up_pre = dot(full_acts, lax.all_gather(w_up, "dp", axis=0, tiled=True))
    back_grad = dot(masked_grad, lax.all_gather(w_down_t, "dp", axis=0, tiled=True))
    hidden, grad_gate, grad_up = activations(gate_pre, up_pre, back_grad)
    proj = jnp.stack(
        [
            outer_sum(dot(full_acts, d_proj[0]), dot(grad_gate, ff_proj[0]), length),
            outer_sum(dot(full_acts, d_proj[1]), dot(grad_up, ff_proj[1]), length),
            outer_sum(dot(hidden, ff_proj[2]), dot(masked_grad, d_proj[2]), length),
        ],
        axis=1,
    )
    proj_b = lax.psum(proj.reshape(seq_dev, 3 * rank * rank), "tensor").astype(jnp.bfloat16)
    flat_scores = lax.dot_general(
        proj_b,
        lax.all_gather(queries, "dp", axis=0, tiled=True),
        (((1,), (1,)), ((), ())),
        preferred_element_type=jnp.float32,
    )
    return flat_scores.reshape(seq_dev, lax.axis_size("dp"), queries.shape[0])


def permute_dp(value, flip):
    return lax.ppermute(value, "dp", [(i, i ^ flip) for i in range(lax.axis_size("dp"))])


def permute_parts(value):
    return lax.ppermute(value, "parts", [(0, 1), (1, 0)])


def hidden_units_kernel(
    places, acts_ref, grad_ref, w_gate, w_up, w_down, near_ref, far_ref, relayed_ref, ff_ref, sums_in, sums_ref
):
    half = far_ref.shape[1] // 2
    depth = w_gate.shape[0]

    def columns(ref, k, size):
        return ref[:, pl.ds(pl.multiple_of(places[k], half), size)]

    def pre(ref, own, m):
        total = dot(columns(ref, 1, depth), own[...])
        total += dot(columns(ref, 2, depth), near_ref[m])
        for k, held in ((3, far_ref), (5, relayed_ref)):
            total += dot(columns(ref, k, half), held[m, :half])
            total += dot(columns(ref, k + 1, half), held[m, half:])
        return total

    hidden, grad_gate, grad_up = activations(pre(acts_ref, w_gate, 0), pre(acts_ref, w_up, 1), pre(grad_ref, w_down, 2))
    rank = ff_ref.shape[2]
    for m, value in enumerate((grad_gate, grad_up, hidden)):
        at = slice(m * rank, (m + 1) * rank)
        sums_ref[:, at] = sums_in[:, at] + dot(value, ff_ref[m])


def add_hidden_units(places, acts, grad, weights, near_rows, far, relayed, ff_proj, sums, tile):
    tokens, model = acts.shape
    depth = weights[0].shape[0]
    chunk = near_rows.shape[2]
    by_tile = lambda i, places: (i, 0)
    own = pl.BlockSpec((depth, chunk), lambda i, places: (0, places[0]))
    whole = lambda v: pl.BlockSpec(v.shape, lambda i, places: (0, 0, 0))
    return pl.pallas_call(
        hidden_units_kernel,
        out_shape=jax.ShapeDtypeStruct(sums.shape, sums.dtype),
        grid_spec=pltpu.PrefetchScalarGridSpec(
            num_scalar_prefetch=1,
            grid=(tokens // tile,),
            in_specs=[
                pl.BlockSpec((tile, model), by_tile),
                pl.BlockSpec((tile, model), by_tile),
                own,
                own,
                own,
                whole(near_rows),
                whole(far),
                whole(relayed),
                pl.BlockSpec((3, chunk, ff_proj.shape[2]), lambda i, places: (0, places[0], 0)),
                pl.BlockSpec((tile, sums.shape[1]), by_tile),
            ],
            out_specs=pl.BlockSpec((tile, sums.shape[1]), by_tile),
        ),
        input_output_aliases={10: 0},
        compiler_params=pltpu.CompilerParams(vmem_limit_bytes=48 * 2**20),
        cost_estimate=pl.CostEstimate(flops=1000, bytes_accessed=1000, transcendentals=0),
    )(places, acts, grad, *weights, near_rows, far, relayed, ff_proj, sums)


def relayed_body(acts, out_grad, lengths, w_gate, w_up, w_down_t, d_proj, ff_proj, queries):
    seq_dev = lengths.shape[0]
    tokens, depth_acts = acts.shape
    length = tokens // seq_dev
    rank = d_proj.shape[2]
    depth = w_gate.shape[0]
    me = lax.axis_index("dp")
    near = lax.rem(me, 2)
    part = lax.axis_index("parts")
    half = w_gate.shape[1] // 2
    chunk = 256
    chunks = half // chunk
    row_half = depth // 2
    weights = (w_gate, w_up, w_down_t)

    def piece(side, j, row_at=0, rows=depth):
        start = side * half + j * chunk
        return jnp.stack([lax.dynamic_slice(w, (row_at, start), (rows, chunk)) for w in weights])

    near_rows, far, relayed = [], [], []
    for j in range(chunks):
        near_rows.append(permute_dp(piece(1 - near, j), 1))
        out = jnp.concatenate(
            [
                piece(near, j, part * row_half, row_half),
                lax.dynamic_slice_in_dim(near_rows[j], part * row_half, row_half, 1),
            ],
            axis=1,
        )
        if j >= 2:
            out, far[j - 2] = lax.optimization_barrier((out, far[j - 2]))
        far.append(permute_dp(out, 2))

    def gathered(value):
        own = lax.all_gather(value, "tensor", axis=1, tiled=True)
        return jnp.concatenate([own, permute_dp(own, 1)], axis=0)

    full_acts = gathered(acts)
    full_grad = gathered(mask_tokens(out_grad, lengths))
    left_both = dot(full_acts, jnp.concatenate([d_proj[0], d_proj[1]], axis=1))
    right_down = dot(full_grad, d_proj[2])
    sums = jnp.zeros((2 * tokens, 3 * rank), jnp.float32)

    def add(j, sums):
        starts = [near * chunks + j, me * depth, (me ^ 1) * depth]
        starts += [(me ^ flip) * depth + side * row_half for side in (part, 1 - part) for flip in (2, 3)]
        places = jnp.stack([jnp.asarray(s, jnp.int32) for s in starts])
        return add_hidden_units(
            places, full_acts, full_grad, weights, near_rows[j], far[j], relayed[j], ff_proj, sums, 256
        )

    gates = {chunks - 2: 2, chunks - 1: 5}
    done = 0
    for j in range(chunks):
        value = far[j]
        if j >= 1:
            value, relayed[j - 1] = lax.optimization_barrier((value, relayed[j - 1]))
        for k in range(done, gates.get(j, done)):
            sums = add(k, sums)
        if gates.get(j, done) > done:
            done = gates[j]
            value, sums = lax.optimization_barrier((value, sums))
        far[j] = value
        relayed.append(permute_parts(value))
    for k in range(done, chunks):
        sums = add(k, sums)
    right_gate, right_up, left_down = jnp.split(sums, 3, axis=1)
    proj = jnp.stack(
        [
            outer_sum(left_both[:, :rank], right_gate, length),
            outer_sum(left_both[:, rank:], right_up, length),
            outer_sum(left_down, right_down, length),
        ],
        axis=1,
    ).reshape(2 * seq_dev, 3 * rank * rank)
    proj = proj[:seq_dev] + permute_dp(proj[seq_dev:], 1)
    proj_b = lax.psum(proj, "tensor").astype(jnp.bfloat16)
    flat_scores = lax.dot_general(
        proj_b,
        lax.all_gather(queries, "dp", axis=0, tiled=True),
        (((1,), (1,)), ((), ())),
        preferred_element_type=jnp.float32,
    )
    return flat_scores.reshape(seq_dev, lax.axis_size("dp"), queries.shape[0])


def solution(mesh):
    in_specs = (
        P(("parts", "dp"), "tensor"),
        P(("parts", "dp"), "tensor"),
        P(("parts", "dp")),
        P("dp", "tensor"),
        P("dp", "tensor"),
        P("dp", "tensor"),
        P(),
        P(None, "tensor", None),
        P(("dp", "tensor"), None),
    )
    out_specs = P(("parts", "dp"), None, "tensor")
    relayed = mesh.shape["dp"] == 4 and mesh.shape["parts"] == 2
    body = relayed_body if relayed else gathered_body
    return jax.shard_map(body, mesh=mesh, in_specs=in_specs, out_specs=out_specs, check_vma=False)
```

```python
import jax
import jax.numpy as jnp
from jax import lax
from jax.experimental import pallas as pl
from jax.experimental.pallas import tpu as pltpu
from jax.sharding import Mesh, PartitionSpec as P

HIGHEST = lax.Precision.HIGHEST


def dot(left, right):
    return jnp.dot(left, right, preferred_element_type=jnp.float32)


def activations(gate_pre, up_pre, back_grad):
    sigmoid_gate = jax.nn.sigmoid(gate_pre)
    silu_gate = gate_pre * sigmoid_gate
    hidden = (silu_gate * up_pre).astype(jnp.bfloat16)
    grad_gate = (
        back_grad * up_pre * sigmoid_gate * (1.0 + gate_pre * (1.0 - sigmoid_gate))
    ).astype(jnp.bfloat16)
    grad_up = (back_grad * silu_gate).astype(jnp.bfloat16)
    return hidden, grad_gate, grad_up


def outer_sum(left, right, length):
    rank = left.shape[1]
    left_seq = left.reshape(-1, length, rank)
    right_seq = right.reshape(-1, length, rank)
    return jnp.einsum("slr,slk->srk", left_seq, right_seq, precision=HIGHEST)


def mask_tokens(out_grad, lengths):
    length = out_grad.shape[0] // lengths.shape[0]
    positions = jnp.arange(length, dtype=jnp.int32)
    keep = positions[None, :] < lengths[:, None]
    return out_grad * keep.astype(out_grad.dtype).reshape(-1, 1)


def gathered_body(acts, out_grad, lengths, w_gate, w_up, w_down_t, d_proj, ff_proj, queries):
    seq_dev = lengths.shape[0]
    length = acts.shape[0] // seq_dev
    rank = d_proj.shape[2]
    full_acts = lax.all_gather(acts, "tensor", axis=1, tiled=True)
    masked_grad = lax.all_gather(mask_tokens(out_grad, lengths), "tensor", axis=1, tiled=True)
    gate_pre = dot(full_acts, lax.all_gather(w_gate, "dp", axis=0, tiled=True))
    up_pre = dot(full_acts, lax.all_gather(w_up, "dp", axis=0, tiled=True))
    back_grad = dot(masked_grad, lax.all_gather(w_down_t, "dp", axis=0, tiled=True))
    hidden, grad_gate, grad_up = activations(gate_pre, up_pre, back_grad)
    proj = jnp.stack(
        [
            outer_sum(dot(full_acts, d_proj[0]), dot(grad_gate, ff_proj[0]), length),
            outer_sum(dot(full_acts, d_proj[1]), dot(grad_up, ff_proj[1]), length),
            outer_sum(dot(hidden, ff_proj[2]), dot(masked_grad, d_proj[2]), length),
        ],
        axis=1,
    )
    proj_b = lax.psum(proj.reshape(seq_dev, 3 * rank * rank), "tensor").astype(jnp.bfloat16)
    flat_scores = lax.dot_general(
        proj_b,
        lax.all_gather(queries, "dp", axis=0, tiled=True),
        (((1,), (1,)), ((), ())),
        preferred_element_type=jnp.float32,
    )
    return flat_scores.reshape(seq_dev, lax.axis_size("dp"), queries.shape[0])


DP = ("far", "near")


def permute_dp(value, flip):
    return lax.ppermute(value, DP, [(i, i ^ flip) for i in range(4)])


def permute_tensor(value, flip):
    return lax.ppermute(value, "tensor", [(i, i ^ flip) for i in range(lax.axis_size("tensor"))])


def permute_parts(value):
    return lax.ppermute(value, "parts", [(0, 1), (1, 0)])


def pre_activation(places, tokens_ref, own, pieces):
    depth = own.shape[0]
    rows = depth // 2

    def columns(k, size):
        at = pl.multiple_of(lax.rem(places[k], depth), rows)
        return tokens_ref[places[k] // depth, :, pl.ds(at, size)]

    total = dot(tokens_ref[places[1] // depth], own[...])
    for k, (ref, plane) in enumerate(pieces):
        total += dot(columns(2 + k, rows), ref[plane])
    return total


def add_projected(sums_in, sums_ref, values, ff_ref):
    rank = ff_ref.shape[1]
    for m, value in enumerate(values):
        at = slice(m * rank, (m + 1) * rank)
        if value is None:
            sums_ref[:, at] = sums_in[:, at]
        else:
            product = lax.dot_general(value, ff_ref[m], (((1,), (1,)), ((), ())), preferred_element_type=jnp.float32)
            sums_ref[:, at] = sums_in[:, at] + product


def direct_kernel(tokens_ref, d_ref, out):
    depth = tokens_ref.shape[2]
    out[...] = sum(dot(tokens_ref[q], d_ref[q * depth : (q + 1) * depth]) for q in range(tokens_ref.shape[0]))


def token_tiles(tokens, near_count, tile):
    per_near = tokens.shape[1] // tile
    shape = (tokens.shape[0] // near_count, tile, tokens.shape[2])
    return pl.BlockSpec(shape, lambda i, *_: (i // per_near, i % per_near, 0)), near_count * per_near


def direct(tokens, d):
    tile = 256
    spec, tiles = token_tiles(tokens, 2, tile)
    return pl.pallas_call(
        direct_kernel,
        out_shape=jax.ShapeDtypeStruct((tiles * tile, d.shape[1]), jnp.float32),
        grid=(tiles,),
        in_specs=[spec, pl.BlockSpec(d.shape, lambda i: (0, 0))],
        out_specs=pl.BlockSpec((tile, d.shape[1]), lambda i: (i, 0)),
        compiler_params=pltpu.CompilerParams(vmem_limit_bytes=48 * 2**20),
        cost_estimate=pl.CostEstimate(flops=1000, bytes_accessed=1000, transcendentals=0),
    )(tokens, d)


def planes(pieces, m):
    return [(ref, m) for ref in pieces]


def both_kernel(places, acts_ref, grad_ref, w_gate, w_up, w_down, *refs):
    *pieces, ff_ref, sums_in, sums_ref = refs
    gate_pre = pre_activation(places, acts_ref, w_gate, planes(pieces, 0))
    up_pre = pre_activation(places, acts_ref, w_up, planes(pieces, 1))
    back_grad = pre_activation(places, grad_ref, w_down, planes(pieces, 2))
    hidden, grad_gate, grad_up = activations(gate_pre, up_pre, back_grad)
    add_projected(sums_in, sums_ref, (grad_gate, grad_up, hidden), ff_ref)


def forward_kernel(places, acts_ref, w_gate, w_up, *refs):
    *pieces, ff_ref, sums_in, sums_ref, gate_factor, up_factor = refs
    gate_pre = pre_activation(places, acts_ref, w_gate, planes(pieces, 0))
    up_pre = pre_activation(places, acts_ref, w_up, planes(pieces, 1))
    sigmoid_gate = jax.nn.sigmoid(gate_pre)
    silu_gate = gate_pre * sigmoid_gate
    gate_factor[...] = up_pre * sigmoid_gate * (1.0 + gate_pre * (1.0 - sigmoid_gate))
    up_factor[...] = silu_gate
    add_projected(sums_in, sums_ref, (None, None, (silu_gate * up_pre).astype(jnp.bfloat16)), ff_ref)


def backward_kernel(places, grad_ref, w_down, *refs):
    *pieces, gate_factor, up_factor, ff_ref, sums_in, sums_ref = refs
    back_grad = pre_activation(places, grad_ref, w_down, planes(pieces, 0))
    grad_gate = (back_grad * gate_factor[...]).astype(jnp.bfloat16)
    grad_up = (back_grad * up_factor[...]).astype(jnp.bfloat16)
    add_projected(sums_in, sums_ref, (grad_gate, grad_up, None), ff_ref)


def add_hidden_units(kernel, places, tokens, weights, pieces, factors, ff_proj, sums):
    tile = 256
    token_spec, tiles = token_tiles(tokens[0], 2, tile)
    rows = tiles * tile
    depth = weights[0].shape[0]
    chunk = pieces[0][0].shape[2]
    by_tile = lambda i, places: (i, 0)
    own = pl.BlockSpec((depth, chunk), lambda i, places: (0, places[0]))
    piece = lambda v, count, block: pl.BlockSpec((count, *v.shape[1:]), lambda i, places: (block, 0, 0))
    factor = pl.BlockSpec((tile, chunk), by_tile)
    total = pl.BlockSpec((tile, sums.shape[1]), by_tile)
    out_shape, out_specs = [jax.ShapeDtypeStruct(sums.shape, sums.dtype)], [total]
    if kernel is forward_kernel:
        out_shape += [jax.ShapeDtypeStruct((rows, chunk), jnp.float32)] * 2
        out_specs += [factor] * 2
    operands = [*tokens, *weights, *(v for v, _, _ in pieces), *factors, ff_proj, sums]
    return pl.pallas_call(
        kernel,
        out_shape=out_shape,
        grid_spec=pltpu.PrefetchScalarGridSpec(
            num_scalar_prefetch=1,
            grid=(tiles,),
            in_specs=[token_spec] * len(tokens)
            + [own] * len(weights)
            + [piece(*p) for p in pieces]
            + [factor] * len(factors)
            + [pl.BlockSpec((3, ff_proj.shape[1], chunk), lambda i, places: (0, 0, places[0])), total],
            out_specs=out_specs,
        ),
        input_output_aliases={len(operands): 0},
        compiler_params=pltpu.CompilerParams(vmem_limit_bytes=48 * 2**20),
        cost_estimate=pl.CostEstimate(flops=1000, bytes_accessed=1000, transcendentals=0),
    )(places, *operands)


def cut_kernel(at, *refs):
    *sources, mine, kept, left = refs
    for m in range(3):
        mine[m] = sources[m][...]
        kept[m] = sources[3 + m][...]
        left[m] = sources[6 + m][...]


def cut(weights, side, mine_at, other_at, rows, chunk):
    tile = 256
    at = jnp.stack([jnp.asarray(v, jnp.int32) for v in (side * rows // tile, (1 - side) * rows // tile, mine_at, other_at)])
    block = lambda r, c: pl.BlockSpec((tile, chunk), lambda i, at: (at[r] + i, at[c]))
    out = pl.BlockSpec((3, tile, chunk), lambda i, at: (0, i, 0))
    return pl.pallas_call(
        cut_kernel,
        out_shape=[jax.ShapeDtypeStruct((3, rows, chunk), weights[0].dtype)] * 3,
        grid_spec=pltpu.PrefetchScalarGridSpec(
            num_scalar_prefetch=1,
            grid=(rows // tile,),
            in_specs=[block(0, 2)] * 3 + [block(0, 3)] * 3 + [block(1, 3)] * 3,
            out_specs=[out] * 3,
        ),
        cost_estimate=pl.CostEstimate(flops=1000, bytes_accessed=1000, transcendentals=0),
    )(at, *weights, *weights, *weights)


def token_kernel(value, out):
    out[...] = value[...]


def token(value):
    block = pl.BlockSpec((8, 128), lambda i: (0, 0))
    return pl.pallas_call(
        token_kernel,
        out_shape=jax.ShapeDtypeStruct((8, 128), value.dtype),
        grid=(1,),
        in_specs=[block],
        out_specs=block,
        cost_estimate=pl.CostEstimate(flops=600000000, bytes_accessed=1000, transcendentals=0),
    )(value)


def after(value, *others):
    return lax.optimization_barrier((value, *others))[0]


def relayed_body(acts, out_grad, lengths, w_gate, w_up, w_down_t, d_proj, ff_proj, queries):
    seq_dev = lengths.shape[0]
    tokens = acts.shape[0]
    length = tokens // seq_dev
    rank = d_proj.shape[2]
    depth = w_gate.shape[0]
    me = lax.axis_index(DP)
    near = lax.axis_index("near")
    part = lax.axis_index("parts")
    half = w_gate.shape[1] // 2
    chunk = 256
    chunks = half // chunk
    rows = depth // 2
    weights = (w_gate, w_up, w_down_t)
    blocks = 2 * chunks
    last = blocks - 1
    ticks, joined = [], {}

    def at(stage, value):
        return after(value, ticks[stage]) if stage >= 0 else value

    def join(stage, *values):
        joined.setdefault(min(stage, last), []).extend(values)

    def end(stage, value):
        ticks.append(after(token(value), *joined[stage]))

    pair = jnp.stack([queries, permute_dp(queries, 2)])
    join(0, pair)
    gathered_acts = lax.all_gather(acts, ("near", "tensor"))
    gathered_grad = lax.all_gather(mask_tokens(out_grad, lengths), ("near", "tensor"))
    sums = jnp.zeros((2 * tokens, 3 * rank), jnp.float32)
    ff_columns = jnp.swapaxes(ff_proj, 1, 2)
    far, relayed, near_rows, cuts = [], [], [], []
    factors = [None] * chunks

    def add(kernel, j, sums):
        starts = [near * chunks + j, me * depth]
        starts += [(me ^ 1) * depth + side * rows for side in (part, 1 - part)]
        starts += [(me ^ flip) * depth + side * rows for side in (part, 1 - part) for flip in (2, 3)]
        places = jnp.stack([jnp.asarray(s, jnp.int32) for s in starts])
        sources = near_rows[j] + far[2 * j : 2 * j + 2] + relayed[2 * j : 2 * j + 2]
        run = lambda *args: add_hidden_units(kernel, places, *args, ff_columns, sums)
        if kernel is forward_kernel:
            sums, *factors[j] = run([full_acts], weights[:2], [(v, 2, 0) for v in sources], [])
        elif kernel is backward_kernel:
            (sums,) = run([full_grad], weights[2:], [(v, 1, 2) for v in sources], factors[j])
        else:
            (sums,) = run([full_acts, full_grad], weights, [(v, 3, 0) for v in sources], [])
        return sums

    def send(g):
        j = g // 2
        if g % 2 == 0:
            sources = [at(g - 3, w) for w in weights]
            cuts.append(cut(sources, part, near * chunks + j, (1 - near) * chunks + j, rows, chunk))
        far.append(permute_dp(at(g - 2, cuts[j][g % 2]), 2 + g % 2))
        join(g, far[g])

    work = {
        6: [(forward_kernel, 0)],
        7: [(forward_kernel, 1)],
        8: [(forward_kernel, 2)],
        9: [(backward_kernel, 0)],
        10: [(forward_kernel, 3)],
        11: [(backward_kernel, 1), (backward_kernel, 2)],
        12: [(forward_kernel, 4)],
        13: [(backward_kernel, 3), (backward_kernel, 4)],
    }
    rest = [(both_kernel, 5), (both_kernel, 6)]
    send(0)
    send(1)
    for g in range(blocks):
        if g in work:
            sums = after(sums, token(ticks[g - 1]))
            for kernel, j in work[g]:
                sums = add(kernel, j, sums)
            end(g, sums)
        else:
            end(g, ticks[-1] if ticks else jnp.zeros((8, 128), jnp.float32))
        relayed.append(permute_parts(at(g, far[g])))
        join(g + 2, relayed[g])
        if g + 2 < blocks:
            send(g + 2)
        if g % 2 == 1:
            near_rows.append([permute_dp(at(g, v), 1) for v in cuts[g // 2][1:]])
            join(g + 2, *near_rows[-1])
        if g == 1:
            near_pair = permute_dp(at(1, pair), 1)
            join(3, near_pair)
        if g == 5:
            full_acts = at(5, gathered_acts)
        if g == 8:
            full_grad = at(8, gathered_grad)
    sums = at(last, sums)
    left_both = direct(at(last, full_acts), jnp.concatenate([d_proj[0], d_proj[1]], axis=1))
    right_down = direct(at(last, full_grad), d_proj[2])
    for kernel, j in rest:
        sums = add(kernel, j, sums)
    right_gate, right_up, left_down = jnp.split(sums, 3, axis=1)
    left_gate, left_up = jnp.split(left_both, 2, axis=1)
    proj = jnp.stack(
        [
            outer_sum(left_gate, right_gate, length),
            outer_sum(left_up, right_up, length),
            outer_sum(left_down, right_down, length),
        ],
        axis=1,
    ).reshape(2, seq_dev, 3 * rank * rank)
    near_proj = permute_dp(lax.dynamic_index_in_dim(proj, 1 - near, 0, False), 1)
    proj = lax.dynamic_index_in_dim(proj, near, 0, False) + near_proj
    sent = proj.astype(jnp.bfloat16)
    for flip in range(1, lax.axis_size("tensor")):
        proj += permute_tensor(sent, flip).astype(jnp.float32)
    flat_scores = lax.dot_general(
        proj.astype(jnp.bfloat16),
        jnp.stack([pair, near_pair]).reshape(4 * queries.shape[0], -1),
        (((1,), (1,)), ((), ())),
        preferred_element_type=jnp.float32,
    )
    blocks = flat_scores.reshape(seq_dev, 4, queries.shape[0])
    order = jnp.stack([me ^ flip for flip in (0, 2, 1, 3)])
    place = (jnp.arange(4)[:, None] == order[None, :]).astype(jnp.float32)
    return jnp.einsum("ak,skc->sac", place, blocks, precision=HIGHEST)


def solution(mesh):
    sizes = mesh.shape
    relayed = sizes["dp"] == 4 and sizes["parts"] == 2 and sizes["tensor"] == 4
    dp = DP if relayed else ("dp",)
    if relayed:
        mesh = Mesh(mesh.devices.reshape(2, 2, 2, 4), ("parts", *DP, "tensor"))
    in_specs = (
        P(("parts", *dp), "tensor"),
        P(("parts", *dp), "tensor"),
        P(("parts", *dp)),
        P(dp, "tensor"),
        P(dp, "tensor"),
        P(dp, "tensor"),
        P(),
        P(None, "tensor", None),
        P((*dp, "tensor"), None),
    )
    out_specs = P(("parts", *dp), None, "tensor")
    body = relayed_body if relayed else gathered_body
    return jax.shard_map(body, mesh=mesh, in_specs=in_specs, out_specs=out_specs, check_vma=False)
```

```python
import jax
import jax.numpy as jnp
from jax import lax
from jax.experimental import pallas as pl
from jax.experimental.pallas import tpu as pltpu
from jax.sharding import Mesh, PartitionSpec as P

HIGHEST = lax.Precision.HIGHEST


def dot(left, right):
    return jnp.dot(left, right, preferred_element_type=jnp.float32)


def dot_rows(left, right):
    return lax.dot_general(left, right, (((1,), (1,)), ((), ())), preferred_element_type=jnp.float32)


def activations(gate_pre, up_pre, back_grad):
    sigmoid_gate = jax.nn.sigmoid(gate_pre)
    silu_gate = gate_pre * sigmoid_gate
    hidden = (silu_gate * up_pre).astype(jnp.bfloat16)
    grad_gate = (
        back_grad * up_pre * sigmoid_gate * (1.0 + gate_pre * (1.0 - sigmoid_gate))
    ).astype(jnp.bfloat16)
    grad_up = (back_grad * silu_gate).astype(jnp.bfloat16)
    return hidden, grad_gate, grad_up


def outer_sum(left, right, length):
    rank = left.shape[1]
    left_seq = left.reshape(-1, length, rank)
    right_seq = right.reshape(-1, length, rank)
    return jnp.einsum("slr,slk->srk", left_seq, right_seq, precision=HIGHEST)


def mask_tokens(out_grad, lengths):
    length = out_grad.shape[0] // lengths.shape[0]
    positions = jnp.arange(length, dtype=jnp.int32)
    keep = positions[None, :] < lengths[:, None]
    return out_grad * keep.astype(out_grad.dtype).reshape(-1, 1)


def gathered_body(acts, out_grad, lengths, w_gate, w_up, w_down_t, d_proj, ff_proj, queries):
    seq_dev = lengths.shape[0]
    length = acts.shape[0] // seq_dev
    rank = d_proj.shape[2]
    full_acts = lax.all_gather(acts, "tensor", axis=1, tiled=True)
    masked_grad = lax.all_gather(mask_tokens(out_grad, lengths), "tensor", axis=1, tiled=True)
    gate_pre = dot(full_acts, lax.all_gather(w_gate, "dp", axis=0, tiled=True))
    up_pre = dot(full_acts, lax.all_gather(w_up, "dp", axis=0, tiled=True))
    back_grad = dot(masked_grad, lax.all_gather(w_down_t, "dp", axis=0, tiled=True))
    hidden, grad_gate, grad_up = activations(gate_pre, up_pre, back_grad)
    proj = jnp.stack(
        [
            outer_sum(dot(full_acts, d_proj[0]), dot(grad_gate, ff_proj[0]), length),
            outer_sum(dot(full_acts, d_proj[1]), dot(grad_up, ff_proj[1]), length),
            outer_sum(dot(hidden, ff_proj[2]), dot(masked_grad, d_proj[2]), length),
        ],
        axis=1,
    )
    proj_b = lax.psum(proj.reshape(seq_dev, 3 * rank * rank), "tensor").astype(jnp.bfloat16)
    flat_scores = lax.dot_general(
        proj_b,
        lax.all_gather(queries, "dp", axis=0, tiled=True),
        (((1,), (1,)), ((), ())),
        preferred_element_type=jnp.float32,
    )
    return flat_scores.reshape(seq_dev, lax.axis_size("dp"), queries.shape[0])


DP = ("far", "near")


def permute_dp(value, flip):
    return lax.ppermute(value, DP, [(i, i ^ flip) for i in range(4)])


def permute_tensor(value, flip):
    return lax.ppermute(value, "tensor", [(i, i ^ flip) for i in range(lax.axis_size("tensor"))])


def permute_parts(value):
    return lax.ppermute(value, "parts", [(0, 1), (1, 0)])


def pre_activation(places, tokens_ref, own, pieces):
    depth = own.shape[0]
    rows = depth // 2

    def columns(k, size):
        at = pl.multiple_of(lax.rem(places[k], depth), rows)
        return tokens_ref[places[k] // depth, :, pl.ds(at, size)]

    total = dot(tokens_ref[places[1] // depth], own[...])
    for k, (ref, plane) in enumerate(pieces):
        total += dot(columns(2 + k, rows), ref[plane])
    return total


def add_projected(sums_in, sums_ref, values, ff_ref):
    rank = ff_ref.shape[1]
    for m, value in enumerate(values):
        at = slice(m * rank, (m + 1) * rank)
        if value is None:
            sums_ref[:, at] = sums_in[:, at]
        else:
            sums_ref[:, at] = sums_in[:, at] + dot_rows(value, ff_ref[m])


def direct_kernel(tokens_ref, d_ref, out):
    count, rank, model = d_ref.shape
    depth = tokens_ref.shape[2]
    for m in range(count):
        total = 0.0
        for q in range(model // depth):
            total += dot_rows(tokens_ref[q], d_ref[m, :, q * depth : (q + 1) * depth])
        out[:, m * rank : (m + 1) * rank] = total


def token_tiles(tokens, near_count, tile):
    per_near = tokens.shape[1] // tile
    shape = (tokens.shape[0] // near_count, tile, tokens.shape[2])
    return pl.BlockSpec(shape, lambda i, *_: (i // per_near, i % per_near, 0)), near_count * per_near


def direct(tokens, d_columns, at, count):
    tile = 256
    spec, tiles = token_tiles(tokens, 2, tile)
    _, rank, model = d_columns.shape
    return pl.pallas_call(
        direct_kernel,
        out_shape=jax.ShapeDtypeStruct((tiles * tile, count * rank), jnp.float32),
        grid=(tiles,),
        in_specs=[spec, pl.BlockSpec((count, rank, model), lambda i: (at // count, 0, 0))],
        out_specs=pl.BlockSpec((tile, count * rank), lambda i: (i, 0)),
        compiler_params=pltpu.CompilerParams(vmem_limit_bytes=48 * 2**20),
        cost_estimate=pl.CostEstimate(flops=1000, bytes_accessed=1000, transcendentals=0),
    )(tokens, d_columns)


def planes(pieces, m):
    return [(ref, m) for ref in pieces]


def both_kernel(places, acts_ref, grad_ref, w_gate, w_up, w_down, *refs):
    *pieces, ff_ref, sums_in, sums_ref = refs
    gate_pre = pre_activation(places, acts_ref, w_gate, planes(pieces, 0))
    up_pre = pre_activation(places, acts_ref, w_up, planes(pieces, 1))
    back_grad = pre_activation(places, grad_ref, w_down, planes(pieces, 2))
    hidden, grad_gate, grad_up = activations(gate_pre, up_pre, back_grad)
    add_projected(sums_in, sums_ref, (grad_gate, grad_up, hidden), ff_ref)


def forward_kernel(places, acts_ref, w_gate, w_up, *refs):
    *pieces, ff_ref, sums_in, sums_ref, gate_factor, up_factor = refs
    gate_pre = pre_activation(places, acts_ref, w_gate, planes(pieces, 0))
    up_pre = pre_activation(places, acts_ref, w_up, planes(pieces, 1))
    sigmoid_gate = jax.nn.sigmoid(gate_pre)
    silu_gate = gate_pre * sigmoid_gate
    gate_factor[...] = up_pre * sigmoid_gate * (1.0 + gate_pre * (1.0 - sigmoid_gate))
    up_factor[...] = silu_gate
    add_projected(sums_in, sums_ref, (None, None, (silu_gate * up_pre).astype(jnp.bfloat16)), ff_ref)


def backward_kernel(places, grad_ref, w_down, *refs):
    *pieces, gate_factor, up_factor, ff_ref, sums_in, sums_ref = refs
    back_grad = pre_activation(places, grad_ref, w_down, planes(pieces, 0))
    grad_gate = (back_grad * gate_factor[...]).astype(jnp.bfloat16)
    grad_up = (back_grad * up_factor[...]).astype(jnp.bfloat16)
    add_projected(sums_in, sums_ref, (grad_gate, grad_up, None), ff_ref)


def add_hidden_units(kernel, places, tokens, weights, pieces, factors, ff_proj, sums):
    tile = 256
    token_spec, tiles = token_tiles(tokens[0], 2, tile)
    rows = tiles * tile
    depth = weights[0].shape[0]
    chunk = pieces[0][0].shape[2]
    by_tile = lambda i, places: (i, 0)
    own = pl.BlockSpec((depth, chunk), lambda i, places: (0, places[0]))
    piece = lambda v, count, block: pl.BlockSpec((count, *v.shape[1:]), lambda i, places: (block, 0, 0))
    factor = pl.BlockSpec((tile, chunk), by_tile)
    total = pl.BlockSpec((tile, sums.shape[1]), by_tile)
    out_shape, out_specs = [jax.ShapeDtypeStruct(sums.shape, sums.dtype)], [total]
    if kernel is forward_kernel:
        out_shape += [jax.ShapeDtypeStruct((rows, chunk), jnp.float32)] * 2
        out_specs += [factor] * 2
    operands = [*tokens, *weights, *(v for v, _, _ in pieces), *factors, ff_proj, sums]
    return pl.pallas_call(
        kernel,
        out_shape=out_shape,
        grid_spec=pltpu.PrefetchScalarGridSpec(
            num_scalar_prefetch=1,
            grid=(tiles,),
            in_specs=[token_spec] * len(tokens)
            + [own] * len(weights)
            + [piece(*p) for p in pieces]
            + [factor] * len(factors)
            + [pl.BlockSpec((3, ff_proj.shape[1], chunk), lambda i, places: (0, 0, places[0])), total],
            out_specs=out_specs,
        ),
        input_output_aliases={len(operands): 0},
        compiler_params=pltpu.CompilerParams(vmem_limit_bytes=48 * 2**20),
        cost_estimate=pl.CostEstimate(flops=1000, bytes_accessed=1000, transcendentals=0),
    )(places, *operands)


def cut_kernel(at, *refs):
    *sources, mine, kept, left = refs
    for m in range(3):
        mine[m] = sources[m][...]
        kept[m] = sources[3 + m][...]
        left[m] = sources[6 + m][...]


def cut(weights, side, mine_at, other_at, rows, chunk):
    tile = 256
    at = jnp.stack([jnp.asarray(v, jnp.int32) for v in (side * rows // tile, (1 - side) * rows // tile, mine_at, other_at)])
    block = lambda r, c: pl.BlockSpec((tile, chunk), lambda i, at: (at[r] + i, at[c]))
    out = pl.BlockSpec((3, tile, chunk), lambda i, at: (0, i, 0))
    return pl.pallas_call(
        cut_kernel,
        out_shape=[jax.ShapeDtypeStruct((3, rows, chunk), weights[0].dtype)] * 3,
        grid_spec=pltpu.PrefetchScalarGridSpec(
            num_scalar_prefetch=1,
            grid=(rows // tile,),
            in_specs=[block(0, 2)] * 3 + [block(0, 3)] * 3 + [block(1, 3)] * 3,
            out_specs=[out] * 3,
        ),
        cost_estimate=pl.CostEstimate(flops=1000, bytes_accessed=1000, transcendentals=0),
    )(at, *weights, *weights, *weights)


def token_kernel(value, out):
    out[...] = value[...]


def token(value):
    block = pl.BlockSpec((8, 128), lambda i: (0, 0))
    return pl.pallas_call(
        token_kernel,
        out_shape=jax.ShapeDtypeStruct((8, 128), value.dtype),
        grid=(1,),
        in_specs=[block],
        out_specs=block,
        cost_estimate=pl.CostEstimate(flops=600000000, bytes_accessed=1000, transcendentals=0),
    )(value)


def after(value, *others):
    return lax.optimization_barrier((value, *others))[0]


def relayed_body(acts, out_grad, lengths, w_gate, w_up, w_down_t, d_proj, ff_proj, queries):
    seq_dev = lengths.shape[0]
    tokens = acts.shape[0]
    length = tokens // seq_dev
    rank = d_proj.shape[2]
    depth = w_gate.shape[0]
    me = lax.axis_index(DP)
    near = lax.axis_index("near")
    part = lax.axis_index("parts")
    half = w_gate.shape[1] // 2
    chunk = 256
    chunks = half // chunk
    rows = depth // 2
    weights = (w_gate, w_up, w_down_t)
    blocks = 2 * chunks
    last = blocks - 1
    ticks, joined = [], {}

    def at(stage, value):
        return after(value, ticks[stage]) if stage >= 0 else value

    def join(stage, *values):
        joined.setdefault(min(stage, last), []).extend(values)

    def end(stage, value):
        ticks.append(after(token(value), *joined[stage]))

    pair = jnp.stack([queries, permute_dp(queries, 2)])
    join(0, pair)
    gathered_acts = lax.all_gather(acts, ("near", "tensor"))
    gathered_grad = lax.all_gather(mask_tokens(out_grad, lengths), ("near", "tensor"))
    sums = jnp.zeros((2 * tokens, 3 * rank), jnp.float32)
    ff_columns, d_columns = jnp.swapaxes(ff_proj, 1, 2), jnp.swapaxes(d_proj, 1, 2)
    far, relayed, near_rows, cuts = [], [], [], []
    factors = [None] * chunks

    def add(kernel, j, sums):
        starts = [near * chunks + j, me * depth]
        starts += [(me ^ 1) * depth + side * rows for side in (part, 1 - part)]
        starts += [(me ^ flip) * depth + side * rows for side in (part, 1 - part) for flip in (2, 3)]
        places = jnp.stack([jnp.asarray(s, jnp.int32) for s in starts])
        sources = near_rows[j] + far[2 * j : 2 * j + 2] + relayed[2 * j : 2 * j + 2]
        run = lambda *args: add_hidden_units(kernel, places, *args, ff_columns, sums)
        if kernel is forward_kernel:
            sums, *factors[j] = run([full_acts], weights[:2], [(v, 2, 0) for v in sources], [])
        elif kernel is backward_kernel:
            (sums,) = run([full_grad], weights[2:], [(v, 1, 2) for v in sources], factors[j])
        else:
            (sums,) = run([full_acts, full_grad], weights, [(v, 3, 0) for v in sources], [])
        return sums

    def make(j):
        sources = [at(j - 2, w) for w in weights]
        cuts.append(cut(sources, part, near * chunks + j, (1 - near) * chunks + j, rows, chunk))
        if j > 0:
            join(j - 1, *cuts[j])

    def send(g):
        far.append(permute_dp(at(g - 2, cuts[g // 2][g % 2]), 2 + g % 2))
        join(g, far[g])

    work = {
        5: [(forward_kernel, 0)],
        6: [(forward_kernel, 1)],
        8: [(forward_kernel, 2)],
        9: [(backward_kernel, 0)],
        10: [(both_kernel, 3)],
        11: [(backward_kernel, 1), (backward_kernel, 2)],
        12: [(both_kernel, 4)],
        13: [(both_kernel, 5)],
    }
    make(0)
    send(0)
    send(1)
    for g in range(blocks):
        if g + 1 < chunks:
            make(g + 1)
        if g in work:
            sums = after(sums, token(ticks[g - 1]))
            for kernel, j in work[g]:
                sums = add(kernel, j, sums)
            end(g, sums)
        elif g == 7:
            left_both = direct(after(full_acts, token(ticks[g - 1])), d_columns, 0, 2)
            end(g, left_both)
        else:
            end(g, ticks[-1] if ticks else jnp.zeros((8, 128), jnp.float32))
        relayed.append(permute_parts(at(min(g, last - 1), far[g])))
        join(g + 2 if g < 10 else g + 1, relayed[g])
        if g + 2 < blocks:
            send(g + 2)
        if g % 2 == 1:
            near_rows.append([permute_dp(at(g, v), 1) for v in cuts[g // 2][1:]])
            join(g + 2, *near_rows[-1])
        if g == 1:
            near_pair = permute_dp(at(1, pair), 1)
            join(3, near_pair)
        if g == 4:
            full_acts = at(4, gathered_acts)
        if g == 8:
            full_grad = at(8, gathered_grad)
    sums = at(last, sums)
    right_down = direct(after(full_grad, sums), d_columns, 2, 1)
    sums = add(both_kernel, 6, after(sums, right_down))
    right_gate, right_up, left_down = jnp.split(sums, 3, axis=1)
    left_gate, left_up = jnp.split(left_both, 2, axis=1)
    proj = jnp.stack(
        [
            outer_sum(left_gate, right_gate, length),
            outer_sum(left_up, right_up, length),
            outer_sum(left_down, right_down, length),
        ],
        axis=1,
    ).reshape(2, seq_dev, 3 * rank * rank)
    near_proj = permute_dp(lax.dynamic_index_in_dim(proj, 1 - near, 0, False), 1)
    proj = lax.dynamic_index_in_dim(proj, near, 0, False) + near_proj
    for flip in (1, 2):
        proj += permute_tensor(proj, flip)
    flat_scores = lax.dot_general(
        proj.astype(jnp.bfloat16),
        jnp.stack([pair, near_pair]).reshape(4 * queries.shape[0], -1),
        (((1,), (1,)), ((), ())),
        preferred_element_type=jnp.float32,
    )
    blocks = flat_scores.reshape(seq_dev, 4, queries.shape[0])
    order = jnp.stack([me ^ flip for flip in (0, 2, 1, 3)])
    place = (jnp.arange(4)[:, None] == order[None, :]).astype(jnp.float32)
    return jnp.einsum("ak,skc->sac", place, blocks, precision=HIGHEST)


def solution(mesh):
    sizes = mesh.shape
    relayed = sizes["dp"] == 4 and sizes["parts"] == 2 and sizes["tensor"] == 4
    dp = DP if relayed else ("dp",)
    if relayed:
        mesh = Mesh(mesh.devices.reshape(2, 2, 2, 4), ("parts", *DP, "tensor"))
    in_specs = (
        P(("parts", *dp), "tensor"),
        P(("parts", *dp), "tensor"),
        P(("parts", *dp)),
        P(dp, "tensor"),
        P(dp, "tensor"),
        P(dp, "tensor"),
        P(),
        P(None, "tensor", None),
        P((*dp, "tensor"), None),
    )
    out_specs = P(("parts", *dp), None, "tensor")
    body = relayed_body if relayed else gathered_body
    return jax.shard_map(body, mesh=mesh, in_specs=in_specs, out_specs=out_specs, check_vma=False)
```

```python
import jax
import jax.numpy as jnp
from jax import lax
from jax.experimental import pallas as pl
from jax.experimental.pallas import tpu as pltpu
from jax.sharding import Mesh, PartitionSpec as P

HIGHEST = lax.Precision.HIGHEST


def dot(left, right):
    return jnp.dot(left, right, preferred_element_type=jnp.float32)


def dot_rows(left, right):
    return lax.dot_general(left, right, (((1,), (1,)), ((), ())), preferred_element_type=jnp.float32)


def activations(gate_pre, up_pre, back_grad):
    sigmoid_gate = jax.nn.sigmoid(gate_pre)
    silu_gate = gate_pre * sigmoid_gate
    hidden = (silu_gate * up_pre).astype(jnp.bfloat16)
    grad_gate = (
        back_grad * up_pre * sigmoid_gate * (1.0 + gate_pre * (1.0 - sigmoid_gate))
    ).astype(jnp.bfloat16)
    grad_up = (back_grad * silu_gate).astype(jnp.bfloat16)
    return hidden, grad_gate, grad_up


def outer_sum(left, right, length):
    rank = left.shape[1]
    left_seq = left.reshape(-1, length, rank)
    right_seq = right.reshape(-1, length, rank)
    return jnp.einsum("slr,slk->srk", left_seq, right_seq, precision=HIGHEST)


def mask_tokens(out_grad, lengths):
    length = out_grad.shape[0] // lengths.shape[0]
    positions = jnp.arange(length, dtype=jnp.int32)
    keep = positions[None, :] < lengths[:, None]
    return out_grad * keep.astype(out_grad.dtype).reshape(-1, 1)


def gathered_body(acts, out_grad, lengths, w_gate, w_up, w_down_t, d_proj, ff_proj, queries):
    seq_dev = lengths.shape[0]
    length = acts.shape[0] // seq_dev
    rank = d_proj.shape[2]
    full_acts = lax.all_gather(acts, "tensor", axis=1, tiled=True)
    masked_grad = lax.all_gather(mask_tokens(out_grad, lengths), "tensor", axis=1, tiled=True)
    gate_pre = dot(full_acts, lax.all_gather(w_gate, "dp", axis=0, tiled=True))
    up_pre = dot(full_acts, lax.all_gather(w_up, "dp", axis=0, tiled=True))
    back_grad = dot(masked_grad, lax.all_gather(w_down_t, "dp", axis=0, tiled=True))
    hidden, grad_gate, grad_up = activations(gate_pre, up_pre, back_grad)
    proj = jnp.stack(
        [
            outer_sum(dot(full_acts, d_proj[0]), dot(grad_gate, ff_proj[0]), length),
            outer_sum(dot(full_acts, d_proj[1]), dot(grad_up, ff_proj[1]), length),
            outer_sum(dot(hidden, ff_proj[2]), dot(masked_grad, d_proj[2]), length),
        ],
        axis=1,
    )
    proj_b = lax.psum(proj.reshape(seq_dev, 3 * rank * rank), "tensor").astype(jnp.bfloat16)
    flat_scores = lax.dot_general(
        proj_b,
        lax.all_gather(queries, "dp", axis=0, tiled=True),
        (((1,), (1,)), ((), ())),
        preferred_element_type=jnp.float32,
    )
    return flat_scores.reshape(seq_dev, lax.axis_size("dp"), queries.shape[0])


DP = ("far", "near")


def permute_dp(value, flip):
    return lax.ppermute(value, DP, [(i, i ^ flip) for i in range(4)])


def permute_tensor(value, flip):
    return lax.ppermute(value, "tensor", [(i, i ^ flip) for i in range(lax.axis_size("tensor"))])


def permute_parts(value):
    return lax.ppermute(value, "parts", [(0, 1), (1, 0)])


def pre_activation(places, tokens_ref, own, pieces):
    depth = own.shape[0]
    rows = depth // 2

    def columns(k, size):
        at = pl.multiple_of(lax.rem(places[k], depth), rows)
        return tokens_ref[places[k] // depth, :, pl.ds(at, size)]

    total = dot(tokens_ref[places[1] // depth], own[...])
    for k, (ref, plane) in enumerate(pieces):
        total += dot(columns(2 + k, rows), ref[plane])
    return total


def add_projected(sums_in, sums_ref, values, ff_ref):
    rank = ff_ref.shape[1]
    for m, value in enumerate(values):
        at = slice(m * rank, (m + 1) * rank)
        if value is None:
            sums_ref[:, at] = sums_in[:, at]
        else:
            sums_ref[:, at] = sums_in[:, at] + dot_rows(value, ff_ref[m])


def direct_kernel(tokens_ref, d_ref, out):
    count, rank, model = d_ref.shape
    depth = tokens_ref.shape[2]
    for m in range(count):
        total = 0.0
        for q in range(model // depth):
            total += dot_rows(tokens_ref[q], d_ref[m, :, q * depth : (q + 1) * depth])
        out[:, m * rank : (m + 1) * rank] = total


def token_tiles(tokens, near_count, tile):
    per_near = tokens.shape[1] // tile
    shape = (tokens.shape[0] // near_count, tile, tokens.shape[2])
    return pl.BlockSpec(shape, lambda i, *_: (i // per_near, i % per_near, 0)), near_count * per_near


def direct(tokens, d_columns, at, count):
    tile = 256
    spec, tiles = token_tiles(tokens, 2, tile)
    _, rank, model = d_columns.shape
    return pl.pallas_call(
        direct_kernel,
        out_shape=jax.ShapeDtypeStruct((tiles * tile, count * rank), jnp.float32),
        grid=(tiles,),
        in_specs=[spec, pl.BlockSpec((count, rank, model), lambda i: (at // count, 0, 0))],
        out_specs=pl.BlockSpec((tile, count * rank), lambda i: (i, 0)),
        compiler_params=pltpu.CompilerParams(vmem_limit_bytes=60 * 2**20),
        cost_estimate=pl.CostEstimate(flops=1000, bytes_accessed=1000, transcendentals=0),
    )(tokens, d_columns)


def planes(pieces, m):
    return [(ref, m) for ref in pieces]


def both_kernel(places, acts_ref, grad_ref, w_gate, w_up, w_down, *refs):
    *pieces, ff_ref, sums_in, sums_ref = refs
    gate_pre = pre_activation(places, acts_ref, w_gate, planes(pieces, 0))
    up_pre = pre_activation(places, acts_ref, w_up, planes(pieces, 1))
    back_grad = pre_activation(places, grad_ref, w_down, planes(pieces, 2))
    hidden, grad_gate, grad_up = activations(gate_pre, up_pre, back_grad)
    add_projected(sums_in, sums_ref, (grad_gate, grad_up, hidden), ff_ref)


def forward_kernel(places, acts_ref, w_gate, w_up, *refs):
    *pieces, ff_ref, sums_in, sums_ref, gate_factor, up_factor = refs
    gate_pre = pre_activation(places, acts_ref, w_gate, planes(pieces, 0))
    up_pre = pre_activation(places, acts_ref, w_up, planes(pieces, 1))
    sigmoid_gate = jax.nn.sigmoid(gate_pre)
    silu_gate = gate_pre * sigmoid_gate
    gate_factor[...] = up_pre * sigmoid_gate * (1.0 + gate_pre * (1.0 - sigmoid_gate))
    up_factor[...] = silu_gate
    add_projected(sums_in, sums_ref, (None, None, (silu_gate * up_pre).astype(jnp.bfloat16)), ff_ref)


def backward_kernel(places, grad_ref, w_down, *refs):
    *pieces, gate_factor, up_factor, ff_ref, sums_in, sums_ref = refs
    back_grad = pre_activation(places, grad_ref, w_down, planes(pieces, 0))
    grad_gate = (back_grad * gate_factor[...]).astype(jnp.bfloat16)
    grad_up = (back_grad * up_factor[...]).astype(jnp.bfloat16)
    add_projected(sums_in, sums_ref, (grad_gate, grad_up, None), ff_ref)


def partial_kernel(places, acts_ref, grad_ref, w_gate, w_up, w_down, *refs):
    *pieces, gate_out, up_out, back_out = refs
    gate_out[...] = pre_activation(places, acts_ref, w_gate, planes(pieces, 0))
    up_out[...] = pre_activation(places, acts_ref, w_up, planes(pieces, 1))
    back_out[...] = pre_activation(places, grad_ref, w_down, planes(pieces, 2))


def last_kernel(places, acts_ref, grad_ref, gate_in, up_in, back_in, piece, ff_ref, sums_in, sums_ref):
    hidden, grad_gate, grad_up = activations(
        gate_in[...] + dot(acts_ref[0], piece[0]),
        up_in[...] + dot(acts_ref[0], piece[1]),
        back_in[...] + dot(grad_ref[0], piece[2]),
    )
    add_projected(sums_in, sums_ref, (grad_gate, grad_up, hidden), ff_ref)


def direct_backward_kernel(places, grad_ref, w_down, *refs):
    *refs, d_ref, ff_ref, sums_in, sums_ref, out = refs
    backward_kernel(places, grad_ref, w_down, *refs, ff_ref, sums_in, sums_ref)
    direct_kernel(grad_ref, d_ref, out)


def small_call(kernel, out_shape, grid, in_specs, out_specs, aliases, operands):
    return pl.pallas_call(
        kernel,
        out_shape=out_shape,
        grid_spec=pltpu.PrefetchScalarGridSpec(
            num_scalar_prefetch=1, grid=grid, in_specs=in_specs, out_specs=out_specs
        ),
        input_output_aliases=aliases,
        compiler_params=pltpu.CompilerParams(vmem_limit_bytes=60 * 2**20),
        cost_estimate=pl.CostEstimate(flops=1000, bytes_accessed=1000, transcendentals=0),
    )(*operands)


def partial_hidden_units(places, tokens, weights, pieces):
    tile = 256
    token_spec, tiles = token_tiles(tokens[0], 2, tile)
    depth, chunk = weights[0].shape[0], pieces[0].shape[2]
    own = pl.BlockSpec((depth, chunk), lambda i, places: (0, places[0]))
    whole = pl.BlockSpec(pieces[0].shape, lambda i, places: (0, 0, 0))
    out = pl.BlockSpec((tile, chunk), lambda i, places: (i, 0))
    return small_call(
        partial_kernel,
        [jax.ShapeDtypeStruct((tiles * tile, chunk), jnp.float32)] * 3,
        (tiles,),
        [token_spec] * 2 + [own] * 3 + [whole] * len(pieces),
        [out] * 3,
        {},
        [places, *tokens, *weights, *pieces],
    )


def last_hidden_units(places, tokens, partial, piece, ff_columns, sums):
    tile = 256
    _, tiles = token_tiles(tokens[0], 2, tile)
    per_near = tiles // 2
    quarters, depth = tokens[0].shape[0] // 2, tokens[0].shape[2]
    rows, chunk = piece.shape[1:]

    def columns(i, places):
        return (i // per_near) * quarters + places[1] // depth, i % per_near, lax.rem(places[1], depth) // rows

    by_tile = lambda i, places: (i, 0)
    total = pl.BlockSpec((tile, sums.shape[1]), by_tile)
    return small_call(
        last_kernel,
        jax.ShapeDtypeStruct(sums.shape, sums.dtype),
        (tiles,),
        [pl.BlockSpec((1, tile, rows), columns)] * 2
        + [pl.BlockSpec((tile, chunk), by_tile)] * 3
        + [
            pl.BlockSpec(piece.shape, lambda i, places: (0, 0, 0)),
            pl.BlockSpec((3, ff_columns.shape[1], chunk), lambda i, places: (0, 0, places[0])),
            total,
        ],
        total,
        {8: 0},
        [places, *tokens, *partial, piece, ff_columns, sums],
    )


def add_hidden_units(kernel, places, tokens, weights, pieces, factors, ff_proj, sums):
    tile = 256
    token_spec, tiles = token_tiles(tokens[0], 2, tile)
    rows = tiles * tile
    depth = weights[0].shape[0]
    chunk = pieces[0][0].shape[2]
    by_tile = lambda i, places: (i, 0)
    own = pl.BlockSpec((depth, chunk), lambda i, places: (0, places[0]))
    piece = lambda v, count, block: pl.BlockSpec((count, *v.shape[1:]), lambda i, places: (block, 0, 0))
    factor = pl.BlockSpec((tile, chunk), by_tile)
    total = pl.BlockSpec((tile, sums.shape[1]), by_tile)
    out_shape, out_specs = [jax.ShapeDtypeStruct(sums.shape, sums.dtype)], [total]
    if kernel is direct_backward_kernel:
        out_shape += [jax.ShapeDtypeStruct((rows, ff_proj.shape[1]), jnp.float32)]
        out_specs += [pl.BlockSpec((tile, ff_proj.shape[1]), by_tile)]
    if kernel is forward_kernel:
        out_shape += [jax.ShapeDtypeStruct((rows, chunk), jnp.float32)] * 2
        out_specs += [factor] * 2
    operands = [*tokens, *weights, *(v for v, _, _ in pieces), *factors, ff_proj, sums]
    return pl.pallas_call(
        kernel,
        out_shape=out_shape,
        grid_spec=pltpu.PrefetchScalarGridSpec(
            num_scalar_prefetch=1,
            grid=(tiles,),
            in_specs=[token_spec] * len(tokens)
            + [own] * len(weights)
            + [piece(*p) for p in pieces]
            + [factor] * 2 * (len(factors) > 1)
            + [pl.BlockSpec((1, *v.shape[1:]), lambda i, places: (2, 0, 0)) for v in factors[2:]]
            + [pl.BlockSpec((3, ff_proj.shape[1], chunk), lambda i, places: (0, 0, places[0])), total],
            out_specs=out_specs,
        ),
        input_output_aliases={len(operands): 0},
        compiler_params=pltpu.CompilerParams(vmem_limit_bytes=60 * 2**20),
        cost_estimate=pl.CostEstimate(flops=1000, bytes_accessed=1000, transcendentals=0),
    )(places, *operands)


def cut_kernel(at, *refs):
    *sources, mine, kept, left = refs
    for m in range(3):
        mine[m] = sources[m][...]
        kept[m] = sources[3 + m][...]
        left[m] = sources[6 + m][...]


def cut(weights, side, mine_at, other_at, rows, chunk):
    tile = 256
    at = jnp.stack([jnp.asarray(v, jnp.int32) for v in (side * rows // tile, (1 - side) * rows // tile, mine_at, other_at)])
    block = lambda r, c: pl.BlockSpec((tile, chunk), lambda i, at: (at[r] + i, at[c]))
    out = pl.BlockSpec((3, tile, chunk), lambda i, at: (0, i, 0))
    return pl.pallas_call(
        cut_kernel,
        out_shape=[jax.ShapeDtypeStruct((3, rows, chunk), weights[0].dtype)] * 3,
        grid_spec=pltpu.PrefetchScalarGridSpec(
            num_scalar_prefetch=1,
            grid=(rows // tile,),
            in_specs=[block(0, 2)] * 3 + [block(0, 3)] * 3 + [block(1, 3)] * 3,
            out_specs=[out] * 3,
        ),
        cost_estimate=pl.CostEstimate(flops=1000, bytes_accessed=1000, transcendentals=0),
    )(at, *weights, *weights, *weights)


def token_kernel(value, out):
    out[...] = value[...]


def token(value):
    block = pl.BlockSpec((8, 128), lambda i: (0, 0))
    return pl.pallas_call(
        token_kernel,
        out_shape=jax.ShapeDtypeStruct((8, 128), value.dtype),
        grid=(1,),
        in_specs=[block],
        out_specs=block,
        cost_estimate=pl.CostEstimate(flops=600000000, bytes_accessed=1000, transcendentals=0),
    )(value)


def after(value, *others):
    return lax.optimization_barrier((value, *others))[0]


def relayed_body(acts, out_grad, lengths, w_gate, w_up, w_down_t, d_proj, ff_proj, queries):
    seq_dev = lengths.shape[0]
    tokens = acts.shape[0]
    length = tokens // seq_dev
    rank = d_proj.shape[2]
    depth = w_gate.shape[0]
    me = lax.axis_index(DP)
    near = lax.axis_index("near")
    part = lax.axis_index("parts")
    half = w_gate.shape[1] // 2
    chunk = 256
    chunks = half // chunk
    rows = depth // 2
    weights = (w_gate, w_up, w_down_t)
    blocks = 2 * chunks
    last = blocks - 1
    ticks, joined = [], {}

    def at(stage, value):
        return after(value, ticks[stage]) if stage >= 0 else value

    def join(stage, *values):
        joined.setdefault(min(stage, last), []).extend(values)

    def end(stage, value):
        ticks.append(after(token(value), *joined[stage]))

    pair = jnp.stack([queries, permute_dp(queries, 2)])
    join(0, pair)
    gathered_acts = lax.all_gather(acts, ("near", "tensor"))
    gathered_grad = lax.all_gather(mask_tokens(out_grad, lengths), ("near", "tensor"))
    sums = jnp.zeros((2 * tokens, 3 * rank), jnp.float32)
    ff_columns, d_columns = jnp.swapaxes(ff_proj, 1, 2), jnp.swapaxes(d_proj, 1, 2)
    far, relayed, near_rows, cuts = [], [], [], []
    factors, rights = [None] * chunks, []

    def places_of(j):
        starts = [near * chunks + j, me * depth]
        starts += [(me ^ 1) * depth + side * rows for side in (part, 1 - part)]
        starts += [(me ^ flip) * depth + side * rows for side in (part, 1 - part) for flip in (2, 3)]
        return jnp.stack([jnp.asarray(s, jnp.int32) for s in starts])

    def add(kernel, j, sums):
        places = places_of(j)
        sources = near_rows[j] + far[2 * j : 2 * j + 2] + relayed[2 * j : 2 * j + 2]
        run = lambda *args: add_hidden_units(kernel, places, *args, ff_columns, sums)
        if kernel is forward_kernel:
            sums, *factors[j] = run([full_acts], weights[:2], [(v, 2, 0) for v in sources], [])
        elif kernel is direct_backward_kernel:
            sums, right_down = run([full_grad], weights[2:], [(v, 1, 2) for v in sources], [*factors[j], d_columns])
            rights.append(right_down)
        elif kernel is backward_kernel:
            (sums,) = run([full_grad], weights[2:], [(v, 1, 2) for v in sources], factors[j])
        else:
            (sums,) = run([full_acts, full_grad], weights, [(v, 3, 0) for v in sources], [])
        return sums

    def make(j):
        sources = [at(j - 2, w) for w in weights]
        cuts.append(cut(sources, part, near * chunks + j, (1 - near) * chunks + j, rows, chunk))
        if j > 0:
            join(j - 1, *cuts[j])

    def send(g):
        far.append(permute_dp(at(g - 2, cuts[g // 2][g % 2]), 2 + g % 2))
        join(g, far[g])

    work = {
        5: [(forward_kernel, 0)],
        6: [(forward_kernel, 1)],
        8: [(forward_kernel, 2)],
        9: [(direct_backward_kernel, 0)],
        10: [(both_kernel, 3)],
        11: [(backward_kernel, 1), (backward_kernel, 2)],
        12: [(both_kernel, 4)],
        13: [(both_kernel, 5)],
    }
    make(0)
    send(0)
    send(1)
    for g in range(blocks):
        if g + 1 < chunks:
            make(g + 1)
        if g in work:
            sums = after(sums, token(ticks[g - 1]))
            for kernel, j in work[g]:
                sums = add(kernel, j, sums)
            end(g, sums)
        elif g == 7:
            left_both = direct(after(full_acts, token(ticks[g - 1])), d_columns, 0, 2)
            end(g, left_both)
        else:
            end(g, ticks[-1] if ticks else jnp.zeros((8, 128), jnp.float32))
        relayed.append(permute_parts(at(min(g, last - 1), far[g])))
        join(g + 2 if g < 10 else g + 1, relayed[g])
        if g + 2 < blocks:
            send(g + 2)
        if g % 2 == 1:
            near_rows.append([permute_dp(at(g, v), 1) for v in cuts[g // 2][1:]])
            join(g + 2, *near_rows[-1])
        if g == 1:
            near_pair = permute_dp(at(1, pair), 1)
            join(3, near_pair)
        if g == 4:
            full_acts = at(4, gathered_acts)
        if g == 8:
            full_grad = at(8, gathered_grad)
    sums = at(last, sums)
    places = places_of(chunks - 1)
    both_tokens = [after(full_acts, sums), full_grad]
    partial = partial_hidden_units(places, both_tokens, weights, near_rows[-1] + far[-2:] + relayed[-2:-1])
    places = jnp.stack([places[0], places[-1]])
    sums = last_hidden_units(places, [full_acts, full_grad], partial, relayed[-1], ff_columns, sums)
    right_gate, right_up, left_down = jnp.split(sums, 3, axis=1)
    left_gate, left_up = jnp.split(left_both, 2, axis=1)
    proj = jnp.stack(
        [
            outer_sum(left_gate, right_gate, length),
            outer_sum(left_up, right_up, length),
            outer_sum(left_down, rights[0], length),
        ],
        axis=1,
    ).reshape(2, seq_dev, 3 * rank * rank)
    near_proj = permute_dp(lax.dynamic_index_in_dim(proj, 1 - near, 0, False), 1)
    proj = lax.dynamic_index_in_dim(proj, near, 0, False) + near_proj
    for flip in (1, 2):
        proj += permute_tensor(proj, flip)
    flat_scores = lax.dot_general(
        proj.astype(jnp.bfloat16),
        jnp.stack([pair, near_pair]).reshape(4 * queries.shape[0], -1),
        (((1,), (1,)), ((), ())),
        preferred_element_type=jnp.float32,
    )
    blocks = flat_scores.reshape(seq_dev, 4, queries.shape[0])
    order = jnp.stack([me ^ flip for flip in (0, 2, 1, 3)])
    place = (jnp.arange(4)[:, None] == order[None, :]).astype(jnp.float32)
    return jnp.einsum("ak,skc->sac", place, blocks, precision=HIGHEST)


def solution(mesh):
    sizes = mesh.shape
    relayed = sizes["dp"] == 4 and sizes["parts"] == 2 and sizes["tensor"] == 4
    dp = DP if relayed else ("dp",)
    if relayed:
        mesh = Mesh(mesh.devices.reshape(2, 2, 2, 4), ("parts", *DP, "tensor"))
    in_specs = (
        P(("parts", *dp), "tensor"),
        P(("parts", *dp), "tensor"),
        P(("parts", *dp)),
        P(dp, "tensor"),
        P(dp, "tensor"),
        P(dp, "tensor"),
        P(),
        P(None, "tensor", None),
        P((*dp, "tensor"), None),
    )
    out_specs = P(("parts", *dp), None, "tensor")
    body = relayed_body if relayed else gathered_body
    return jax.shard_map(body, mesh=mesh, in_specs=in_specs, out_specs=out_specs, check_vma=False)
```

```python
import jax
import jax.numpy as jnp
from jax import lax
from jax.experimental import pallas as pl
from jax.experimental.pallas import tpu as pltpu
from jax.sharding import Mesh, PartitionSpec as P

HIGHEST = lax.Precision.HIGHEST


def dot(left, right):
    return jnp.dot(left, right, preferred_element_type=jnp.float32)


def dot_rows(left, right):
    return lax.dot_general(left, right, (((1,), (1,)), ((), ())), preferred_element_type=jnp.float32)


def activations(gate_pre, up_pre, back_grad):
    sigmoid_gate = jax.nn.sigmoid(gate_pre)
    silu_gate = gate_pre * sigmoid_gate
    hidden = (silu_gate * up_pre).astype(jnp.bfloat16)
    grad_gate = (
        back_grad * up_pre * sigmoid_gate * (1.0 + gate_pre * (1.0 - sigmoid_gate))
    ).astype(jnp.bfloat16)
    grad_up = (back_grad * silu_gate).astype(jnp.bfloat16)
    return hidden, grad_gate, grad_up


def outer_sum(left, right, length):
    rank = left.shape[1]
    left_seq = left.reshape(-1, length, rank)
    right_seq = right.reshape(-1, length, rank)
    return jnp.einsum("slr,slk->srk", left_seq, right_seq, precision=lax.Precision.HIGH)


def mask_tokens(out_grad, lengths):
    length = out_grad.shape[0] // lengths.shape[0]
    positions = jnp.arange(length, dtype=jnp.int32)
    keep = positions[None, :] < lengths[:, None]
    return out_grad * keep.astype(out_grad.dtype).reshape(-1, 1)


def gathered_body(acts, out_grad, lengths, w_gate, w_up, w_down_t, d_proj, ff_proj, queries):
    seq_dev = lengths.shape[0]
    length = acts.shape[0] // seq_dev
    rank = d_proj.shape[2]
    full_acts = lax.all_gather(acts, "tensor", axis=1, tiled=True)
    masked_grad = lax.all_gather(mask_tokens(out_grad, lengths), "tensor", axis=1, tiled=True)
    gate_pre = dot(full_acts, lax.all_gather(w_gate, "dp", axis=0, tiled=True))
    up_pre = dot(full_acts, lax.all_gather(w_up, "dp", axis=0, tiled=True))
    back_grad = dot(masked_grad, lax.all_gather(w_down_t, "dp", axis=0, tiled=True))
    hidden, grad_gate, grad_up = activations(gate_pre, up_pre, back_grad)
    proj = jnp.stack(
        [
            outer_sum(dot(full_acts, d_proj[0]), dot(grad_gate, ff_proj[0]), length),
            outer_sum(dot(full_acts, d_proj[1]), dot(grad_up, ff_proj[1]), length),
            outer_sum(dot(hidden, ff_proj[2]), dot(masked_grad, d_proj[2]), length),
        ],
        axis=1,
    )
    proj_b = lax.psum(proj.reshape(seq_dev, 3 * rank * rank), "tensor").astype(jnp.bfloat16)
    flat_scores = lax.dot_general(
        proj_b,
        lax.all_gather(queries, "dp", axis=0, tiled=True),
        (((1,), (1,)), ((), ())),
        preferred_element_type=jnp.float32,
    )
    return flat_scores.reshape(seq_dev, lax.axis_size("dp"), queries.shape[0])


DP = ("far", "near")


def permute_dp(value, flip):
    return lax.ppermute(value, DP, [(i, i ^ flip) for i in range(4)])


def permute_tensor(value, flip):
    return lax.ppermute(value, "tensor", [(i, i ^ flip) for i in range(lax.axis_size("tensor"))])


def permute_parts(value):
    return lax.ppermute(value, "parts", [(0, 1), (1, 0)])


def pre_activation(places, tokens_ref, own, pieces):
    depth = own.shape[0]
    rows = depth // 2

    def columns(k, size):
        at = pl.multiple_of(lax.rem(places[k], depth), rows)
        return tokens_ref[places[k] // depth, :, pl.ds(at, size)]

    total = dot(tokens_ref[places[1] // depth], own[...])
    for k, (ref, plane) in enumerate(pieces):
        total += dot(columns(2 + k, rows), ref[plane])
    return total


def add_projected(sums_in, sums_ref, values, ff_ref):
    rank = ff_ref.shape[1]
    for m, value in enumerate(values):
        at = slice(m * rank, (m + 1) * rank)
        if value is None:
            sums_ref[:, at] = sums_in[:, at]
        else:
            sums_ref[:, at] = sums_in[:, at] + dot_rows(value, ff_ref[m])


def direct_kernel(tokens_ref, d_ref, out):
    count, rank, model = d_ref.shape
    depth = tokens_ref.shape[2]
    for m in range(count):
        total = 0.0
        for q in range(model // depth):
            total += dot_rows(tokens_ref[q], d_ref[m, :, q * depth : (q + 1) * depth])
        out[:, m * rank : (m + 1) * rank] = total


def token_tiles(tokens, near_count, tile):
    per_near = tokens.shape[1] // tile
    shape = (tokens.shape[0] // near_count, tile, tokens.shape[2])
    return pl.BlockSpec(shape, lambda i, *_: (i // per_near, i % per_near, 0)), near_count * per_near


def direct(tokens, d_columns, at, count):
    tile = 256
    spec, tiles = token_tiles(tokens, 2, tile)
    _, rank, model = d_columns.shape
    return pl.pallas_call(
        direct_kernel,
        out_shape=jax.ShapeDtypeStruct((tiles * tile, count * rank), jnp.float32),
        grid=(tiles,),
        in_specs=[spec, pl.BlockSpec((count, rank, model), lambda i: (at // count, 0, 0))],
        out_specs=pl.BlockSpec((tile, count * rank), lambda i: (i, 0)),
        compiler_params=pltpu.CompilerParams(vmem_limit_bytes=60 * 2**20),
        cost_estimate=pl.CostEstimate(flops=1000, bytes_accessed=1000, transcendentals=0),
    )(tokens, d_columns)


def planes(pieces, m):
    return [(ref, m) for ref in pieces]


def both_kernel(places, acts_ref, grad_ref, w_gate, w_up, w_down, *refs):
    *pieces, ff_ref, sums_in, sums_ref = refs
    gate_pre = pre_activation(places, acts_ref, w_gate, planes(pieces, 0))
    up_pre = pre_activation(places, acts_ref, w_up, planes(pieces, 1))
    back_grad = pre_activation(places, grad_ref, w_down, planes(pieces, 2))
    hidden, grad_gate, grad_up = activations(gate_pre, up_pre, back_grad)
    add_projected(sums_in, sums_ref, (grad_gate, grad_up, hidden), ff_ref)


def forward_kernel(places, acts_ref, w_gate, w_up, *refs):
    *pieces, ff_ref, sums_in, sums_ref, gate_factor, up_factor = refs
    gate_pre = pre_activation(places, acts_ref, w_gate, planes(pieces, 0))
    up_pre = pre_activation(places, acts_ref, w_up, planes(pieces, 1))
    sigmoid_gate = jax.nn.sigmoid(gate_pre)
    silu_gate = gate_pre * sigmoid_gate
    gate_factor[...] = up_pre * sigmoid_gate * (1.0 + gate_pre * (1.0 - sigmoid_gate))
    up_factor[...] = silu_gate
    add_projected(sums_in, sums_ref, (None, None, (silu_gate * up_pre).astype(jnp.bfloat16)), ff_ref)


def backward_kernel(places, grad_ref, w_down, *refs):
    *pieces, gate_factor, up_factor, ff_ref, sums_in, sums_ref = refs
    back_grad = pre_activation(places, grad_ref, w_down, planes(pieces, 0))
    grad_gate = (back_grad * gate_factor[...]).astype(jnp.bfloat16)
    grad_up = (back_grad * up_factor[...]).astype(jnp.bfloat16)
    add_projected(sums_in, sums_ref, (grad_gate, grad_up, None), ff_ref)


def partial_kernel(places, acts_ref, grad_ref, w_gate, w_up, w_down, *refs):
    *pieces, gate_out, up_out, back_out = refs
    gate_out[...] = pre_activation(places, acts_ref, w_gate, planes(pieces, 0))
    up_out[...] = pre_activation(places, acts_ref, w_up, planes(pieces, 1))
    back_out[...] = pre_activation(places, grad_ref, w_down, planes(pieces, 2))


def last_kernel(places, acts_ref, grad_ref, gate_in, up_in, back_in, piece, ff_ref, sums_in, sums_ref):
    hidden, grad_gate, grad_up = activations(
        gate_in[...] + dot(acts_ref[0], piece[0]),
        up_in[...] + dot(acts_ref[0], piece[1]),
        back_in[...] + dot(grad_ref[0], piece[2]),
    )
    add_projected(sums_in, sums_ref, (grad_gate, grad_up, hidden), ff_ref)


def direct_backward_kernel(places, grad_ref, w_down, *refs):
    *refs, d_ref, ff_ref, sums_in, sums_ref, out = refs
    backward_kernel(places, grad_ref, w_down, *refs, ff_ref, sums_in, sums_ref)
    direct_kernel(grad_ref, d_ref, out)


def small_call(kernel, out_shape, grid, in_specs, out_specs, aliases, operands):
    return pl.pallas_call(
        kernel,
        out_shape=out_shape,
        grid_spec=pltpu.PrefetchScalarGridSpec(
            num_scalar_prefetch=1, grid=grid, in_specs=in_specs, out_specs=out_specs
        ),
        input_output_aliases=aliases,
        compiler_params=pltpu.CompilerParams(vmem_limit_bytes=60 * 2**20),
        cost_estimate=pl.CostEstimate(flops=1000, bytes_accessed=1000, transcendentals=0),
    )(*operands)


def partial_hidden_units(places, tokens, weights, pieces):
    tile = 256
    token_spec, tiles = token_tiles(tokens[0], 2, tile)
    depth, chunk = weights[0].shape[0], pieces[0].shape[2]
    own = pl.BlockSpec((depth, chunk), lambda i, places: (0, places[0]))
    whole = pl.BlockSpec(pieces[0].shape, lambda i, places: (0, 0, 0))
    out = pl.BlockSpec((tile, chunk), lambda i, places: (i, 0))
    return small_call(
        partial_kernel,
        [jax.ShapeDtypeStruct((tiles * tile, chunk), jnp.float32)] * 3,
        (tiles,),
        [token_spec] * 2 + [own] * 3 + [whole] * len(pieces),
        [out] * 3,
        {},
        [places, *tokens, *weights, *pieces],
    )


def last_hidden_units(places, tokens, partial, piece, ff_columns, sums):
    tile = 256
    _, tiles = token_tiles(tokens[0], 2, tile)
    per_near = tiles // 2
    quarters, depth = tokens[0].shape[0] // 2, tokens[0].shape[2]
    rows, chunk = piece.shape[1:]

    def columns(i, places):
        return (i // per_near) * quarters + places[1] // depth, i % per_near, lax.rem(places[1], depth) // rows

    by_tile = lambda i, places: (i, 0)
    total = pl.BlockSpec((tile, sums.shape[1]), by_tile)
    return small_call(
        last_kernel,
        jax.ShapeDtypeStruct(sums.shape, sums.dtype),
        (tiles,),
        [pl.BlockSpec((1, tile, rows), columns)] * 2
        + [pl.BlockSpec((tile, chunk), by_tile)] * 3
        + [
            pl.BlockSpec(piece.shape, lambda i, places: (0, 0, 0)),
            pl.BlockSpec((3, ff_columns.shape[1], chunk), lambda i, places: (0, 0, places[0])),
            total,
        ],
        total,
        {8: 0},
        [places, *tokens, *partial, piece, ff_columns, sums],
    )


def add_hidden_units(kernel, places, tokens, weights, pieces, factors, ff_proj, sums):
    tile = 256
    token_spec, tiles = token_tiles(tokens[0], 2, tile)
    rows = tiles * tile
    depth = weights[0].shape[0]
    chunk = pieces[0][0].shape[2]
    by_tile = lambda i, places: (i, 0)
    own = pl.BlockSpec((depth, chunk), lambda i, places: (0, places[0]))
    piece = lambda v, count, block: pl.BlockSpec((count, *v.shape[1:]), lambda i, places: (block, 0, 0))
    factor = pl.BlockSpec((tile, chunk), by_tile)
    total = pl.BlockSpec((tile, sums.shape[1]), by_tile)
    out_shape, out_specs = [jax.ShapeDtypeStruct(sums.shape, sums.dtype)], [total]
    if kernel is direct_backward_kernel:
        out_shape += [jax.ShapeDtypeStruct((rows, ff_proj.shape[1]), jnp.float32)]
        out_specs += [pl.BlockSpec((tile, ff_proj.shape[1]), by_tile)]
    if kernel is forward_kernel:
        out_shape += [jax.ShapeDtypeStruct((rows, chunk), jnp.float32)] * 2
        out_specs += [factor] * 2
    operands = [*tokens, *weights, *(v for v, _, _ in pieces), *factors, ff_proj, sums]
    return pl.pallas_call(
        kernel,
        out_shape=out_shape,
        grid_spec=pltpu.PrefetchScalarGridSpec(
            num_scalar_prefetch=1,
            grid=(tiles,),
            in_specs=[token_spec] * len(tokens)
            + [own] * len(weights)
            + [piece(*p) for p in pieces]
            + [factor] * 2 * (len(factors) > 1)
            + [pl.BlockSpec((1, *v.shape[1:]), lambda i, places: (2, 0, 0)) for v in factors[2:]]
            + [pl.BlockSpec((3, ff_proj.shape[1], chunk), lambda i, places: (0, 0, places[0])), total],
            out_specs=out_specs,
        ),
        input_output_aliases={len(operands): 0},
        compiler_params=pltpu.CompilerParams(vmem_limit_bytes=60 * 2**20),
        cost_estimate=pl.CostEstimate(flops=1000, bytes_accessed=1000, transcendentals=0),
    )(places, *operands)


def cut_kernel(at, *refs):
    *sources, mine, kept, left = refs
    for m in range(3):
        mine[m] = sources[m][...]
        kept[m] = sources[3 + m][...]
        left[m] = sources[6 + m][...]


def cut(weights, side, mine_at, other_at, rows, chunk):
    tile = 256
    at = jnp.stack([jnp.asarray(v, jnp.int32) for v in (side * rows // tile, (1 - side) * rows // tile, mine_at, other_at)])
    block = lambda r, c: pl.BlockSpec((tile, chunk), lambda i, at: (at[r] + i, at[c]))
    out = pl.BlockSpec((3, tile, chunk), lambda i, at: (0, i, 0))
    return pl.pallas_call(
        cut_kernel,
        out_shape=[jax.ShapeDtypeStruct((3, rows, chunk), weights[0].dtype)] * 3,
        grid_spec=pltpu.PrefetchScalarGridSpec(
            num_scalar_prefetch=1,
            grid=(rows // tile,),
            in_specs=[block(0, 2)] * 3 + [block(0, 3)] * 3 + [block(1, 3)] * 3,
            out_specs=[out] * 3,
        ),
        cost_estimate=pl.CostEstimate(flops=1000, bytes_accessed=1000, transcendentals=0),
    )(at, *weights, *weights, *weights)


def token_kernel(value, out):
    out[...] = value[...]


def token(value):
    block = pl.BlockSpec((8, 128), lambda i: (0, 0))
    return pl.pallas_call(
        token_kernel,
        out_shape=jax.ShapeDtypeStruct((8, 128), value.dtype),
        grid=(1,),
        in_specs=[block],
        out_specs=block,
        cost_estimate=pl.CostEstimate(flops=600000000, bytes_accessed=1000, transcendentals=0),
    )(value)


def after(value, *others):
    return lax.optimization_barrier((value, *others))[0]


def relayed_body(acts, out_grad, lengths, w_gate, w_up, w_down_t, d_proj, ff_proj, queries):
    seq_dev = lengths.shape[0]
    tokens = acts.shape[0]
    length = tokens // seq_dev
    rank = d_proj.shape[2]
    depth = w_gate.shape[0]
    me = lax.axis_index(DP)
    near = lax.axis_index("near")
    part = lax.axis_index("parts")
    half = w_gate.shape[1] // 2
    chunk = 256
    chunks = half // chunk
    rows = depth // 2
    weights = (w_gate, w_up, w_down_t)
    blocks = 2 * chunks
    last = blocks - 1
    ticks, joined = [], {}

    def at(stage, value):
        return after(value, ticks[stage]) if stage >= 0 else value

    def join(stage, *values):
        joined.setdefault(min(stage, last), []).extend(values)

    def end(stage, value):
        ticks.append(after(token(value), *joined[stage]))

    pair = jnp.stack([queries, permute_dp(queries, 2)])
    join(0, pair)
    gathered_acts = lax.all_gather(acts, ("near", "tensor"))
    gathered_grad = lax.all_gather(mask_tokens(out_grad, lengths), ("near", "tensor"))
    sums = jnp.zeros((2 * tokens, 3 * rank), jnp.float32)
    ff_columns, d_columns = jnp.swapaxes(ff_proj, 1, 2), jnp.swapaxes(d_proj, 1, 2)
    far, relayed, near_rows, cuts = [], [], [], []
    factors, rights = [None] * chunks, []

    def places_of(j):
        starts = [near * chunks + j, me * depth]
        starts += [(me ^ 1) * depth + side * rows for side in (part, 1 - part)]
        starts += [(me ^ flip) * depth + side * rows for side in (part, 1 - part) for flip in (2, 3)]
        return jnp.stack([jnp.asarray(s, jnp.int32) for s in starts])

    def add(kernel, j, sums):
        places = places_of(j)
        sources = near_rows[j] + far[2 * j : 2 * j + 2] + relayed[2 * j : 2 * j + 2]
        run = lambda *args: add_hidden_units(kernel, places, *args, ff_columns, sums)
        if kernel is forward_kernel:
            sums, *factors[j] = run([full_acts], weights[:2], [(v, 2, 0) for v in sources], [])
        elif kernel is direct_backward_kernel:
            sums, right_down = run([full_grad], weights[2:], [(v, 1, 2) for v in sources], [*factors[j], d_columns])
            rights.append(right_down)
        elif kernel is backward_kernel:
            (sums,) = run([full_grad], weights[2:], [(v, 1, 2) for v in sources], factors[j])
        else:
            (sums,) = run([full_acts, full_grad], weights, [(v, 3, 0) for v in sources], [])
        return sums

    def make(j):
        sources = [at(j - 2, w) for w in weights]
        cuts.append(cut(sources, part, near * chunks + j, (1 - near) * chunks + j, rows, chunk))
        if j > 0:
            join(j - 1, *cuts[j])

    def send(g):
        far.append(permute_dp(at(g - 2, cuts[g // 2][g % 2]), 2 + g % 2))
        join(g, far[g])

    work = {
        5: [(forward_kernel, 0)],
        6: [(forward_kernel, 1)],
        8: [(forward_kernel, 2)],
        9: [(direct_backward_kernel, 0)],
        10: [(both_kernel, 3)],
        11: [(backward_kernel, 1), (backward_kernel, 2)],
        12: [(both_kernel, 4)],
        13: [(both_kernel, 5)],
    }
    make(0)
    send(0)
    send(1)
    for g in range(blocks):
        if g + 1 < chunks:
            make(g + 1)
        if g in work:
            sums = after(sums, token(ticks[g - 1]))
            for kernel, j in work[g]:
                sums = add(kernel, j, sums)
            end(g, sums)
        elif g == 7:
            left_both = direct(after(full_acts, token(ticks[g - 1])), d_columns, 0, 2)
            end(g, left_both)
        else:
            end(g, ticks[-1] if ticks else jnp.zeros((8, 128), jnp.float32))
        relayed.append(permute_parts(at(min(g, last - 1), far[g])))
        join(g + 2 if g < 10 else g + 1, relayed[g])
        if g + 2 < blocks:
            send(g + 2)
        if g % 2 == 1:
            near_rows.append([permute_dp(at(g, v), 1) for v in cuts[g // 2][1:]])
            join(g + 2, *near_rows[-1])
        if g == 1:
            near_pair = permute_dp(at(1, pair), 1)
            join(3, near_pair)
        if g == 4:
            full_acts = at(4, gathered_acts)
        if g == 8:
            full_grad = at(8, gathered_grad)
    sums = at(last, sums)
    places = places_of(chunks - 1)
    both_tokens = [after(full_acts, sums), full_grad]
    partial = partial_hidden_units(places, both_tokens, weights, near_rows[-1] + far[-2:] + relayed[-2:-1])
    places = jnp.stack([places[0], places[-1]])
    sums = last_hidden_units(places, [full_acts, full_grad], partial, relayed[-1], ff_columns, sums)
    right_gate, right_up, left_down = jnp.split(sums, 3, axis=1)
    left_gate, left_up = jnp.split(left_both, 2, axis=1)
    proj = jnp.stack(
        [
            outer_sum(left_gate, right_gate, length),
            outer_sum(left_up, right_up, length),
            outer_sum(left_down, rights[0], length),
        ],
        axis=1,
    ).reshape(2, seq_dev, 3 * rank * rank)
    near_proj = permute_dp(lax.dynamic_index_in_dim(proj, 1 - near, 0, False), 1)
    proj = lax.dynamic_index_in_dim(proj, near, 0, False) + near_proj
    for flip in (1, 2):
        proj += permute_tensor(proj, flip)
    flat_scores = lax.dot_general(
        proj.astype(jnp.bfloat16),
        jnp.stack([pair, near_pair]).reshape(4 * queries.shape[0], -1),
        (((1,), (1,)), ((), ())),
        preferred_element_type=jnp.float32,
    )
    blocks = flat_scores.reshape(seq_dev, 4, queries.shape[0])
    order = jnp.stack([me ^ flip for flip in (0, 2, 1, 3)])
    place = (jnp.arange(4)[:, None] == order[None, :]).astype(jnp.float32)
    return jnp.einsum("ak,skc->sac", place, blocks, precision=HIGHEST)


def solution(mesh):
    sizes = mesh.shape
    relayed = sizes["dp"] == 4 and sizes["parts"] == 2 and sizes["tensor"] == 4
    dp = DP if relayed else ("dp",)
    if relayed:
        mesh = Mesh(mesh.devices.reshape(2, 2, 2, 4), ("parts", *DP, "tensor"))
    in_specs = (
        P(("parts", *dp), "tensor"),
        P(("parts", *dp), "tensor"),
        P(("parts", *dp)),
        P(dp, "tensor"),
        P(dp, "tensor"),
        P(dp, "tensor"),
        P(),
        P(None, "tensor", None),
        P((*dp, "tensor"), None),
    )
    out_specs = P(("parts", *dp), None, "tensor")
    body = relayed_body if relayed else gathered_body
    return jax.shard_map(body, mesh=mesh, in_specs=in_specs, out_specs=out_specs, check_vma=False)
```
